32 devices in a mesh: groups: 2 (over y), ctx: 4 (over z), tp: 4 (over x, core).
Axes of the slice: x: 2, y: 2, z: 4, core: 2. Of those that a mesh axis runs over, the one named last changes fastest.
Arguments:
- hidden: bfloat16 [1024, 8192], P(('groups', 'ctx'), 'tp'), parts along dimension 0, may hold values from -6 to 6
- base_query_rows: bfloat16 [1024, 8192], P(('groups', 'ctx'), 'tp'), parts along dimension 0, may hold values from -60 to 60
- base_key_rows: bfloat16 [1024, 1024], P(('groups', 'ctx'), 'tp'), parts along dimension 0, may hold values from -60 to 60
- base_value_rows: bfloat16 [1024, 1024], P(('groups', 'ctx'), 'tp'), parts along dimension 0, may hold values from -6 to 6
- stored_block_order: int32 [16], P('groups'), parts along dimension 0, may hold values from 0 to 7, each once
- version: int32 [8], P('groups'), parts along dimension 0, may hold values from 0 to 3
- publisher: int32 [2], P('groups'), parts along dimension 0, may hold values from 0 to 3
- adapter_down_weight: bfloat16 [4, 4, 192, 8192], P('ctx', None, None, 'tp'), may hold values from -0.0625 to 0.0625
- adapter_up_query: bfloat16 [4, 4, 64, 8192], P('ctx', None, None, 'tp'), may hold values from -0.75 to 0.75
- adapter_up_key_value: bfloat16 [4, 4, 2, 64, 1024], P('ctx', None, None, None, 'tp'), may hold values from -0.75 to 0.75
- output_down_weight: bfloat16 [4, 4, 64, 8192], P('ctx', None, None, 'tp'), may hold values from -0.1875 to 0.1875
- output_up_weight: bfloat16 [4, 4, 64, 8192], P('ctx', None, None, 'tp'), may hold values from -0.75 to 0.75
Outputs:
- attended: bfloat16 [1024, 8192], P(('groups', 'ctx'), 'tp'), parts along dimension 0
- adapted: bfloat16 [1024, 8192], P(('groups', 'ctx'), 'tp'), parts along dimension 0
The draws below stay inside these ranges and needn't reach their ends.
There are 2 independent parts, one for each index of `groups`. The reference program is written for one: setup_inputs(seed, part) draws one part's arguments, and reference() takes and returns one part's arrays. A program takes and returns all parts, laid end to end along the dimension named above; an argument that names none is the same for every part. Nothing has to cross between parts.
Inputs may be any that keep to these rules, and one draw needn't show every extreme that they name: `stored_block_order`: each half-block of the prompt is stored exactly once.
All inputs are finite; a program needn't handle non-finite values.
Results may differ from the reference program's by a relative error of at most 0.015.
The reference program's roundings to bfloat16 on the way count: a program that leaves them out, or rounds other values in their place, can miss the bound.
Values may be sent and summed in bfloat16 or wider, within the bound.
A program may use at most 64 MiB of HBM per device.

```python
import jax
import jax.numpy as jnp
from jax import lax

MODEL_WIDTH = 8192
QUERY_HEADS = 64
KEY_VALUE_HEADS = 8
HEAD_SIZE = 128
ADAPTER_RANK = 64
SLOT_VERSIONS = 4
PROMPT_TOKENS = 512
HBLK = 64
BLOCKS = 8
N_CTX = 4


def draw_base_query_rows(key, part):
    base_output = jnp.clip(1.6 * jax.random.normal(jax.random.fold_in(key, 11), (PROMPT_TOKENS, QUERY_HEADS, HEAD_SIZE), jnp.float32), -9.0, 9.0)
    return base_output.reshape(PROMPT_TOKENS, QUERY_HEADS * HEAD_SIZE).astype(jnp.bfloat16)


def draw_base_key_rows(key, part):
    base_output = jnp.clip(1.6 * jax.random.normal(jax.random.fold_in(key, 21), (PROMPT_TOKENS, KEY_VALUE_HEADS, HEAD_SIZE), jnp.float32), -9.0, 9.0)
    return base_output.reshape(PROMPT_TOKENS, KEY_VALUE_HEADS * HEAD_SIZE).astype(jnp.bfloat16)


def touch_ends(entries, key, low, high):
    shape = entries.shape
    spot = [jax.random.randint(jax.random.fold_in(key, axis), (), 0, shape[axis]) for axis in range(len(shape))]
    entries = entries.at[tuple(spot)].set(low)
    longest = shape.index(max(shape))
    spot[longest] = (spot[longest] + 1) % shape[longest]
    return entries.at[tuple(spot)].set(high)


def levels(own_key, dims, shards, low, high):
    def one(position, blocks):
        draws = jax.random.uniform(jax.random.fold_in(jax.random.fold_in(own_key, 6), position), (blocks,), jnp.float32, low / len(shards), high / len(shards))
        return jnp.repeat(jnp.exp(draws), dims[position] // blocks).reshape((-1,) + (1,) * (len(dims) - position - 1))

    gain = one(*shards[0])
    for cut in shards[1:]:
        gain = gain * one(*cut)
    return gain


def bell_draw(own_key, extent, scale, bound, split=(), kind=jnp.bfloat16):
    result = jax.random.normal(own_key, extent, jnp.float32) * scale
    if len(split) > 0:
        result = levels(own_key, extent, split, -0.22, 0.18) * result
    return jnp.clip(result, min=-bound, max=bound).astype(kind)


def setup_inputs(seed: int = 0, part: int = 0) -> dict:
    key_of = jax.random.split(jax.random.key(seed), 13)
    part_keys = jax.random.split(jax.random.fold_in(key_of[12], part), 13)
    return {
        "hidden": bell_draw(part_keys[0], (PROMPT_TOKENS, MODEL_WIDTH), 1.0, 6.0, ((0, 4), (1, 4))),
        "base_query_rows": draw_base_query_rows(jax.random.fold_in(jax.random.fold_in(key_of[12], part), 71), part),
        "base_key_rows": draw_base_key_rows(jax.random.fold_in(jax.random.fold_in(key_of[12], part), 71), part),
        "base_value_rows": bell_draw(part_keys[3], (PROMPT_TOKENS, KEY_VALUE_HEADS * HEAD_SIZE), 1.0, 6.0, ((0, 4), (1, 4))),
        "stored_block_order": jax.random.permutation(part_keys[4], BLOCKS).astype(jnp.int32),
        "version": touch_ends(jax.random.randint(part_keys[5], (N_CTX,), 0, SLOT_VERSIONS), jax.random.fold_in(part_keys[5], 1), 0, SLOT_VERSIONS - 1).astype(jnp.int32),
        "publisher": jax.random.randint(part_keys[6], (1,), 0, N_CTX).astype(jnp.int32),
        "adapter_down_weight": bell_draw(key_of[7], (N_CTX, SLOT_VERSIONS, 3 * ADAPTER_RANK, MODEL_WIDTH), MODEL_WIDTH ** -0.5, 0.0625, ((0, 4), (3, 4))),
        "adapter_up_query": bell_draw(key_of[8], (N_CTX, SLOT_VERSIONS, ADAPTER_RANK, QUERY_HEADS * HEAD_SIZE), ADAPTER_RANK ** -0.5, 0.75, ((0, 4), (3, 4))),
        "adapter_up_key_value": bell_draw(key_of[9], (N_CTX, SLOT_VERSIONS, 2, ADAPTER_RANK, KEY_VALUE_HEADS * HEAD_SIZE), ADAPTER_RANK ** -0.5, 0.75, ((0, 4), (4, 4))),
        "output_down_weight": bell_draw(key_of[10], (N_CTX, SLOT_VERSIONS, ADAPTER_RANK, QUERY_HEADS * HEAD_SIZE), (QUERY_HEADS * HEAD_SIZE // 8) ** -0.5, 0.1875, ((0, 4), (3, 4))),
        "output_up_weight": bell_draw(key_of[11], (N_CTX, SLOT_VERSIONS, ADAPTER_RANK, MODEL_WIDTH), ADAPTER_RANK ** -0.5, 0.75, ((0, 4), (3, 4))),
    }


NEG_BIG = -1.0e30


def apply_rotation(values, token_index_list):
    half_dim = values.shape[-1] // 2
    frequency = 500000.0 ** (-(jnp.arange(half_dim, dtype=jnp.float32) * 2.0) / values.shape[-1])
    angles = token_index_list.astype(jnp.float32)[:, None] * frequency[None, :]
    cosine = jnp.cos(angles)[:, None, :]
    sine_part = jnp.sin(angles)[:, None, :]
    first_half = values[..., :half_dim]
    second_half = values[..., half_dim:]
    return jnp.concatenate([first_half * cosine - second_half * sine_part, second_half * cosine + first_half * sine_part], axis=-1)


def token_positions(stored_block_order):
    flat_index = jnp.arange(PROMPT_TOKENS, dtype=jnp.int32)
    return stored_block_order[flat_index // HBLK] * HBLK + flat_index % HBLK


def reference(hidden, base_query_rows, base_key_rows, base_value_rows, stored_block_order, version, publisher, adapter_down_weight, adapter_up_query, adapter_up_key_value, output_down_weight, output_up_weight):
    source_block = publisher[0]
    chosen_version = version[source_block]
    down_output = adapter_down_weight[source_block, chosen_version]
    rank_projection = jnp.dot(hidden, down_output.T, preferred_element_type=jnp.float32).astype(jnp.bfloat16)
    token_index_list = token_positions(stored_block_order)
    adapted_queries = base_query_rows.astype(jnp.float32) + jnp.dot(rank_projection[:, :ADAPTER_RANK], adapter_up_query[source_block, chosen_version], preferred_element_type=jnp.float32)
    adapted_queries = apply_rotation(adapted_queries.reshape(PROMPT_TOKENS, QUERY_HEADS, HEAD_SIZE), token_index_list).astype(jnp.bfloat16)
    adapted_key_rows = base_key_rows.astype(jnp.float32) + jnp.dot(rank_projection[:, ADAPTER_RANK:2 * ADAPTER_RANK], adapter_up_key_value[source_block, chosen_version, 0], preferred_element_type=jnp.float32)
    adapted_key_rows = apply_rotation(adapted_key_rows.reshape(PROMPT_TOKENS, KEY_VALUE_HEADS, HEAD_SIZE), token_index_list).astype(jnp.bfloat16)
    adapted_value_rows = base_value_rows.astype(jnp.float32) + jnp.dot(rank_projection[:, 2 * ADAPTER_RANK:], adapter_up_key_value[source_block, chosen_version, 1], preferred_element_type=jnp.float32)
    adapted_value_rows = adapted_value_rows.astype(jnp.bfloat16).reshape(PROMPT_TOKENS, KEY_VALUE_HEADS, HEAD_SIZE)
    query_group_size = QUERY_HEADS // KEY_VALUE_HEADS
    head_queries = jnp.transpose(adapted_queries, (1, 0, 2))
    head_keys = jnp.repeat(jnp.transpose(adapted_key_rows, (1, 0, 2)), query_group_size, axis=0)
    head_values = jnp.repeat(jnp.transpose(adapted_value_rows, (1, 0, 2)), query_group_size, axis=0)
    visible = token_index_list[None, :] <= token_index_list[:, None]

    def one_head(operands):
        query_head, key_head, value_head = operands
        scores = jnp.dot(query_head, key_head.T, preferred_element_type=jnp.float32) * (HEAD_SIZE ** -0.5)
        scores = jnp.where(visible, scores, NEG_BIG)
        row_max = jnp.max(scores, axis=1, keepdims=True)
        raw_scores = jnp.where(visible, jnp.exp(scores - row_max), 0.0)
        totals = jnp.sum(raw_scores, axis=1)
        mixed = jnp.dot(raw_scores.astype(jnp.bfloat16), value_head, preferred_element_type=jnp.float32)
        return (mixed / totals[:, None]).astype(jnp.bfloat16)

    attended = lax.map(one_head, (head_queries, head_keys, head_values))
    attended = jnp.transpose(attended, (1, 0, 2)).reshape(PROMPT_TOKENS, QUERY_HEADS * HEAD_SIZE)
    out_low = jnp.dot(attended, output_down_weight[source_block, chosen_version].T, preferred_element_type=jnp.float32).astype(jnp.bfloat16)
    adapted = jnp.dot(out_low, output_up_weight[source_block, chosen_version], preferred_element_type=jnp.float32).astype(jnp.bfloat16)
    return attended, adapted
```

```python
import functools

import jax
import jax.numpy as jnp
import numpy as np
from jax import lax
from jax.experimental import pallas as pl
from jax.experimental.pallas import tpu as pltpu
from jax.sharding import PartitionSpec as P

HEAD_SIZE = 128
ADAPTER_RANK = 64
NEG_BIG = -1e30
NT = (((1,), (1,)), ((), ()))
PARTS = 8


def kernel(
    n,
    tp,
    group_size,
    order_ref,
    version_ref,
    publisher_ref,
    frequency_ref,
    hidden_hbm,
    base_q_hbm,
    base_k_hbm,
    base_v_hbm,
    down_hbm,
    up_q_hbm,
    up_kv_hbm,
    outer_down_hbm,
    outer_up_hbm,
    attended_ref,
    adapted_ref,
    hidden,
    base_q,
    base_k,
    base_v,
    own,
    in_r,
    in_l,
    out_r,
    out_l,
    final,
    queries,
    kv_all,
    bias,
    cosine,
    sine,
    partial,
    rs_buf,
    rank_low,
    partial2,
    rs_buf2,
    out_low,
    own_sem,
    base_sem,
    send_r,
    recv_r,
    send_l,
    recv_l,
    kv_send,
    kv_recv,
    rs_send,
    rs_recv,
    ag_send,
    ag_recv,
    rs2_send,
    rs2_recv,
    ag2_send,
    ag2_recv,
):
    me = lax.axis_index("ctx")
    lane = lax.axis_index("tp")
    count, _, rank, cw = own.shape
    rows, width = hidden.shape
    parts = width // cw
    n_down = down_hbm.shape[2] // rank
    first_k = n_down * parts
    first_q = first_k + 2
    first_od = first_q + parts
    first_ou = first_od + parts
    heads_per_chunk = cw // HEAD_SIZE
    groups = kv_all.shape[1] // 2
    share = rows // tp

    def own_copy(src, c):
        return pltpu.make_async_copy(src, own.at[c], own_sem.at[c])

    def cols(k):
        return pl.ds(pl.multiple_of(k * cw, cw), cw)

    def load_down(k, _):
        for r in range(n_down):
            own_copy(
                down_hbm.at[0, :, pl.ds(r * rank, rank), cols(k)], k * n_down + r
            ).start()
        return 0

    base_copies = [
        pltpu.make_async_copy(src, dst, base_sem.at[i])
        for i, (src, dst) in enumerate(
            [(hidden_hbm, hidden), (base_q_hbm, base_q), (base_k_hbm, base_k), (base_v_hbm, base_v)]
        )
    ]

    barrier = pltpu.get_barrier_semaphore()

    def greet(axis, own_index, size):
        def one(d, _):
            pl.semaphore_signal(
                barrier,
                inc=1,
                device_id={axis: lax.rem(own_index + d, size)},
                device_id_type=pl.DeviceIdType.MESH,
            )
            return 0

        lax.fori_loop(1, size, one, 0)

    greet("ctx", me, n)
    greet("tp", lane, tp)

    load_down(0, 0)
    base_copies[0].start()
    lax.fori_loop(1, parts, load_down, 0)
    for c in range(2):
        own_copy(up_kv_hbm.at[0, :, c], first_k + c).start()

    def load_wide(k, _):
        own_copy(up_q_hbm.at[0, :, :, cols(k)], first_q + k).start()
        own_copy(outer_down_hbm.at[0, :, :, cols(k)], first_od + k).start()
        own_copy(outer_up_hbm.at[0, :, :, cols(k)], first_ou + k).start()
        return 0

    lax.fori_loop(0, parts, load_wide, 0)
    for copy in base_copies[1:]:
        copy.start()

    source = publisher_ref[0]
    chosen = version_ref[source]
    is_source = source == me
    from_left = source <= me

    pl.semaphore_wait(barrier, n - 1 + tp - 1)

    def hop_right(c):
        return pltpu.make_async_remote_copy(
            src_ref=out_r.at[c],
            dst_ref=in_r.at[c],
            send_sem=send_r.at[c],
            recv_sem=recv_r.at[c],
            device_id={"ctx": lax.rem(me + 1, n)},
            device_id_type=pl.DeviceIdType.MESH,
        )

    def hop_left(c):
        return pltpu.make_async_remote_copy(
            src_ref=out_l.at[c],
            dst_ref=in_l.at[c],
            send_sem=send_l.at[c],
            recv_sem=recv_l.at[c],
            device_id={"ctx": lax.rem(me + n - 1, n)},
            device_id_type=pl.DeviceIdType.MESH,
        )

    def stored_chunk(c):
        value = own[c, 0]
        for e in range(1, own.shape[1]):
            value = jnp.where(chosen == e, own[c, e], value)
        return value

    def relay(t):
        @pl.when(t < count)
        def _():
            own_copy(own.at[t], t).wait()

        right = t - me

        @pl.when((right >= 0) & (right < count))
        def _():
            @pl.when(me == 0)
            def _():
                out_r[right] = stored_chunk(right)

            @pl.when(me > 0)
            def _():
                hop_right(right).wait_recv()
                out_r[right] = jnp.where(is_source, stored_chunk(right), in_r[right])

            @pl.when(me < n - 1)
            def _():
                hop_right(right).start()

        left = t - (n - 1 - me)

        @pl.when((left >= 0) & (left < count))
        def _():
            @pl.when(me == n - 1)
            def _():
                out_l[left] = stored_chunk(left)

            @pl.when(me < n - 1)
            def _():
                hop_left(left).wait_recv()
                out_l[left] = jnp.where(is_source, stored_chunk(left), in_l[left])

            @pl.when(me > 0)
            def _():
                hop_left(left).start()

        done = t - (n - 1)

        @pl.when(done >= 0)
        def _():
            final[done] = jnp.where(from_left, out_r[done], out_l[done])

    def relay_range(start, stop):
        def one(t, _):
            relay(t)
            return 0

        lax.fori_loop(start, stop, one, 0)

    def tp_copy(src, dst, send, recv, d, sem):
        return pltpu.make_async_remote_copy(
            src_ref=src,
            dst_ref=dst,
            send_sem=send.at[d],
            recv_sem=recv.at[sem],
            device_id={"tp": lax.rem(lane + d, tp)},
            device_id_type=pl.DeviceIdType.MESH,
        )

    def row_share(j):
        return pl.ds(pl.multiple_of(j * share, share), share)

    def each_peer(fn):
        def one(d, _):
            fn(d, lax.rem(lane + d, tp))
            return 0

        lax.fori_loop(1, tp, one, 0)

    def scatter_start(src, buf, send, recv):
        each_peer(
            lambda d, j: tp_copy(
                src.at[row_share(j)], buf.at[lane], send, recv, d, lane
            ).start()
        )
        buf[lane] = src[row_share(lane)]

    def scatter_wait(src, buf, send, recv):
        each_peer(
            lambda d, j: tp_copy(
                src.at[row_share(j)], buf.at[j], send, recv, d, j
            ).wait()
        )
        return jnp.sum(buf[...], axis=0)

    def gather_start(value, buf, send, recv):
        mine = buf.at[row_share(lane)]
        mine[...] = value.astype(buf.dtype)
        each_peer(lambda d, j: tp_copy(mine, mine, send, recv, d, lane).start())

    def gather_wait(buf, send, recv):
        each_peer(
            lambda d, j: tp_copy(
                buf.at[row_share(lane)], buf.at[row_share(j)], send, recv, d, j
            ).wait()
        )

    relay_range(0, n - 1)
    blocks = order_ref.shape[0]
    block_rows = rows * n // blocks
    per_device = blocks // n
    token = lax.broadcasted_iota(jnp.int32, (rows, HEAD_SIZE), 0)
    stored = jnp.zeros((rows, HEAD_SIZE), jnp.int32)
    for b in range(per_device):
        stored = jnp.where(
            token // block_rows == b, order_ref[me * per_device + b], stored
        )
    position = stored * block_rows + token % block_rows
    angle = position.astype(jnp.float32) * frequency_ref[...]
    half = lax.broadcasted_iota(jnp.int32, (rows, HEAD_SIZE), 1) < HEAD_SIZE // 2
    cosine[...] = jnp.cos(angle)
    sine_all = jnp.sin(angle)
    sine[...] = jnp.where(half, -sine_all, sine_all)
    key = lax.broadcasted_iota(jnp.int32, (rows, block_rows * 2), 1)
    query_position = jnp.concatenate(
        [position] * (block_rows * 2 // HEAD_SIZE), axis=1
    )
    for b in range(0, blocks, 2):
        key_position = (
            jnp.where(key < block_rows, order_ref[b], order_ref[b + 1]) * block_rows
            + key % block_rows
        )
        bias[:, b * block_rows : (b + 2) * block_rows] = jnp.where(
            key_position <= query_position, 0.0, NEG_BIG
        )
    partial[...] = jnp.zeros_like(partial)
    partial2[...] = jnp.zeros_like(partial2)
    base_copies[0].wait()

    def down_step(k, _):
        for r in range(n_down):
            relay(n - 1 + k * n_down + r)
        weight = final[pl.ds(k * n_down, n_down)].reshape(n_down * rank, cw)
        partial[:, : n_down * rank] += lax.dot_general(
            hidden[:, cols(k)], weight, NT, preferred_element_type=jnp.float32
        )
        return 0

    lax.fori_loop(0, parts, down_step, 0)
    t = n - 1 + first_k
    scatter_start(partial, rs_buf, rs_send, rs_recv)
    relay_range(t, t + 2)
    gather_start(
        scatter_wait(partial, rs_buf, rs_send, rs_recv), rank_low, ag_send, ag_recv
    )
    relay_range(t + 2, t + 4)
    for copy in base_copies[1:]:
        copy.wait()
    gather_wait(rank_low, ag_send, ag_recv)

    def rotate(values):
        return values * cosine[...] + pltpu.roll(values, HEAD_SIZE // 2, 1) * sine[...]

    low = rank_low[...]
    keys = base_k[...].astype(jnp.float32) + jnp.dot(
        low[:, rank : 2 * rank], final[first_k], preferred_element_type=jnp.float32
    )
    values = base_v[...].astype(jnp.float32) + jnp.dot(
        low[:, 2 * rank : 3 * rank],
        final[first_k + 1],
        preferred_element_type=jnp.float32,
    )
    for g in range(groups):
        span = slice(g * HEAD_SIZE, (g + 1) * HEAD_SIZE)
        kv_all[me, g] = rotate(keys[:, span]).astype(jnp.bfloat16)
        kv_all[me, groups + g] = values[:, span].astype(jnp.bfloat16)

    def kv_copy(d, place):
        return pltpu.make_async_remote_copy(
            src_ref=kv_all.at[me],
            dst_ref=kv_all.at[place],
            send_sem=kv_send.at[d],
            recv_sem=kv_recv.at[place],
            device_id={"ctx": lax.rem(me + d, n)},
            device_id_type=pl.DeviceIdType.MESH,
        )

    def kv_start(d, _):
        kv_copy(d, me).start()
        return 0

    def kv_wait(d, _):
        kv_copy(d, lax.rem(me + d, n)).wait()
        return 0

    lax.fori_loop(1, n, kv_start, 0)

    low_q = low[:, :rank]

    def query_step(j, _):
        relay(t + 4 + j)
        adapted_q = base_q[:, cols(j)].astype(jnp.float32) + jnp.dot(
            low_q, final[first_q + j], preferred_element_type=jnp.float32
        )
        for h in range(heads_per_chunk):
            span = slice(h * HEAD_SIZE, (h + 1) * HEAD_SIZE)
            queries[j, :, span] = rotate(adapted_q[:, span]).astype(jnp.bfloat16)
        return 0

    lax.fori_loop(0, parts, query_step, 0)
    relay_range(t + 4 + parts, n - 1 + first_ou)
    lax.fori_loop(1, n, kv_wait, 0)

    def head_step(j, _):
        relay(n - 1 + first_ou + j)
        for h in range(heads_per_chunk):
            span = slice(h * HEAD_SIZE, (h + 1) * HEAD_SIZE)
            group = (j * heads_per_chunk + h) // group_size
            key_block = kv_all[:, group].reshape(n * rows, HEAD_SIZE)
            value_block = kv_all[:, groups + group].reshape(n * rows, HEAD_SIZE)
            scores = (
                lax.dot_general(
                    queries[j, :, span], key_block, NT, preferred_element_type=jnp.float32
                )
                * HEAD_SIZE ** (-0.5)
                + bias[...]
            )
            raw = jnp.exp(scores - jnp.max(scores, axis=1, keepdims=True))
            totals = jnp.sum(raw, axis=1, keepdims=True)
            mixed = jnp.dot(
                raw.astype(jnp.bfloat16), value_block, preferred_element_type=jnp.float32
            )
            place = pl.ds(pl.multiple_of(j * cw + h * HEAD_SIZE, HEAD_SIZE), HEAD_SIZE)
            attended_ref[:, place] = (mixed / totals).astype(jnp.bfloat16)
        partial2[:, :rank] += lax.dot_general(
            attended_ref[:, cols(j)],
            final[first_od + j],
            NT,
            preferred_element_type=jnp.float32,
        )
        return 0

    lax.fori_loop(0, parts, head_step, 0)
    scatter_start(partial2, rs_buf2, rs2_send, rs2_recv)
    gather_start(
        scatter_wait(partial2, rs_buf2, rs2_send, rs2_recv), out_low, ag2_send, ag2_recv
    )

    def drain(c, _):
        @pl.when(me < n - 1)
        def _():
            hop_right(c).wait_send()

        @pl.when(me > 0)
        def _():
            hop_left(c).wait_send()

        return 0

    lax.fori_loop(0, count, drain, 0)
    gather_wait(out_low, ag2_send, ag2_recv)
    outer = out_low[:, :rank]

    def up_step(j, _):
        adapted_ref[:, cols(j)] = jnp.dot(
            outer, final[first_ou + j], preferred_element_type=jnp.float32
        ).astype(jnp.bfloat16)
        return 0

    lax.fori_loop(0, parts, up_step, 0)


def shards(
    n,
    tp,
    hidden,
    base_query_rows,
    base_key_rows,
    base_value_rows,
    stored_block_order,
    version,
    publisher,
    adapter_down_weight,
    adapter_up_query,
    adapter_up_key_value,
    output_down_weight,
    output_up_weight,
):
    rows, width = hidden.shape
    versions, rank = adapter_up_query.shape[1:3]
    kv_width = base_key_rows.shape[1]
    groups = kv_width // HEAD_SIZE
    cw = width // PARTS
    count = adapter_down_weight.shape[2] // rank * PARTS + 2 + 3 * PARTS
    half = np.arange(HEAD_SIZE // 2, dtype=np.float32) * np.float32(2.0) / np.float32(HEAD_SIZE)
    frequency = np.power(np.float32(500000.0), -half).astype(np.float32)
    frequency = jnp.asarray(np.concatenate([frequency, frequency])[None, :])
    bf16, f32 = jnp.bfloat16, jnp.float32
    chunk = pltpu.VMEM((count, rank, cw), bf16)
    dma = pltpu.SemaphoreType.DMA
    share = rows // tp
    smem = pl.BlockSpec(memory_space=pltpu.SMEM)
    vmem = pl.BlockSpec(memory_space=pltpu.VMEM)
    hbm = pl.BlockSpec(memory_space=pl.ANY)
    out = jax.ShapeDtypeStruct((rows, width), bf16)
    return pl.pallas_call(
        functools.partial(kernel, n, tp, width // kv_width),
        out_shape=(out, out),
        in_specs=[smem] * 3 + [vmem] + [hbm] * 9,
        out_specs=(vmem, vmem),
        scratch_shapes=[
            pltpu.VMEM((rows, width), bf16),
            pltpu.VMEM((rows, width), bf16),
            pltpu.VMEM((rows, kv_width), bf16),
            pltpu.VMEM((rows, kv_width), bf16),
            pltpu.VMEM((count, versions, rank, cw), bf16),
            chunk,
            chunk,
            chunk,
            chunk,
            chunk,
            pltpu.VMEM((PARTS, rows, cw), bf16),
            pltpu.VMEM((n, 2 * groups, rows, HEAD_SIZE), bf16),
            pltpu.VMEM((rows, n * rows), f32),
            pltpu.VMEM((rows, HEAD_SIZE), f32),
            pltpu.VMEM((rows, HEAD_SIZE), f32),
            pltpu.VMEM((rows, 2 * HEAD_SIZE), f32),
            pltpu.VMEM((tp, share, 2 * HEAD_SIZE), f32),
            pltpu.VMEM((rows, 2 * HEAD_SIZE), bf16),
            pltpu.VMEM((rows, HEAD_SIZE), f32),
            pltpu.VMEM((tp, share, HEAD_SIZE), f32),
            pltpu.VMEM((rows, HEAD_SIZE), bf16),
            dma((count,)),
            dma((4,)),
            dma((count,)),
            dma((count,)),
            dma((count,)),
            dma((count,)),
            dma((n,)),
            dma((n,)),
        ]
        + [dma((tp,))] * 8,
        compiler_params=pltpu.CompilerParams(
            collective_id=0, has_side_effects=True, vmem_limit_bytes=48 * 1024 * 1024
        ),
    )(
        stored_block_order,
        version,
        publisher,
        frequency,
        hidden,
        base_query_rows,
        base_key_rows,
        base_value_rows,
        adapter_down_weight,
        adapter_up_query,
        adapter_up_key_value,
        output_down_weight,
        output_up_weight,
    )


def solution(mesh):
    placed = (
        P(("groups", "ctx"), "tp"),
        P(("groups", "ctx"), "tp"),
        P(("groups", "ctx"), "tp"),
        P(("groups", "ctx"), "tp"),
        P("groups"),
        P("groups"),
        P("groups"),
        P("ctx", None, None, "tp"),
        P("ctx", None, None, "tp"),
        P("ctx", None, None, None, "tp"),
        P("ctx", None, None, "tp"),
        P("ctx", None, None, "tp"),
    )
    return jax.shard_map(
        functools.partial(shards, mesh.shape["ctx"], mesh.shape["tp"]),
        mesh=mesh,
        in_specs=placed,
        out_specs=(P(("groups", "ctx"), "tp"), P(("groups", "ctx"), "tp")),
        check_vma=False,
    )
```

```python
import functools

import jax
import jax.numpy as jnp
import numpy as np
from jax import lax
from jax.experimental import pallas as pl
from jax.experimental.pallas import tpu as pltpu
from jax.sharding import PartitionSpec as P

HEAD_SIZE = 128
ADAPTER_RANK = 64
NEG_BIG = -1e30
NT = (((1,), (1,)), ((), ()))
PARTS = 8
LAG = 4


def kernel(
    n,
    tp,
    group_size,
    order_ref,
    version_ref,
    publisher_ref,
    frequency_ref,
    hidden_hbm,
    base_q_hbm,
    base_k_hbm,
    base_v_hbm,
    down_hbm,
    up_q_hbm,
    up_kv_hbm,
    outer_down_hbm,
    outer_up_hbm,
    attended_ref,
    adapted_ref,
    hidden,
    base_q,
    base_k,
    base_v,
    own,
    in_r,
    in_l,
    out_r,
    out_l,
    final,
    queries,
    kv_all,
    bias,
    cosine,
    sine,
    partial,
    rs_buf,
    rank_low,
    partial2,
    rs_buf2,
    out_low,
    own_sem,
    base_sem,
    send_r,
    recv_r,
    send_l,
    recv_l,
    kv_send,
    kv_recv,
    rs_send,
    rs_recv,
    ag_send,
    ag_recv,
    rs2_send,
    rs2_recv,
    ag2_send,
    ag2_recv,
):
    me = lax.axis_index("ctx")
    lane = lax.axis_index("tp")
    count, _, rank, cw = own.shape
    rows, width = hidden.shape
    parts = width // cw
    n_down = down_hbm.shape[2] // rank
    first_k = n_down * parts
    first_q = first_k + 2
    first_od = first_q + parts
    first_ou = first_od + parts
    heads_per_chunk = cw // HEAD_SIZE
    groups = kv_all.shape[1] // 2
    share = rows // tp
    fill = (n - 1) * LAG

    def own_copy(src, c):
        return pltpu.make_async_copy(src, own.at[c], own_sem.at[c])

    def cols(k):
        return pl.ds(pl.multiple_of(k * cw, cw), cw)

    def load_down(k, _):
        for r in range(n_down):
            own_copy(
                down_hbm.at[0, :, pl.ds(r * rank, rank), cols(k)], k * n_down + r
            ).start()
        return 0

    base_copies = [
        pltpu.make_async_copy(src, dst, base_sem.at[i])
        for i, (src, dst) in enumerate(
            [(hidden_hbm, hidden), (base_q_hbm, base_q), (base_k_hbm, base_k), (base_v_hbm, base_v)]
        )
    ]

    barrier = pltpu.get_barrier_semaphore()

    def greet(axis, own_index, size):
        def one(d, _):
            pl.semaphore_signal(
                barrier,
                inc=1,
                device_id={axis: lax.rem(own_index + d, size)},
                device_id_type=pl.DeviceIdType.MESH,
            )
            return 0

        lax.fori_loop(1, size, one, 0)

    greet("ctx", me, n)
    greet("tp", lane, tp)

    load_down(0, 0)
    base_copies[0].start()
    lax.fori_loop(1, parts, load_down, 0)
    for c in range(2):
        own_copy(up_kv_hbm.at[0, :, c], first_k + c).start()

    def load_wide(k, _):
        own_copy(up_q_hbm.at[0, :, :, cols(k)], first_q + k).start()
        own_copy(outer_down_hbm.at[0, :, :, cols(k)], first_od + k).start()
        own_copy(outer_up_hbm.at[0, :, :, cols(k)], first_ou + k).start()
        return 0

    lax.fori_loop(0, parts, load_wide, 0)
    for copy in base_copies[1:]:
        copy.start()

    source = publisher_ref[0]
    chosen = version_ref[source]
    is_source = source == me
    from_left = source <= me

    pl.semaphore_wait(barrier, n - 1 + tp - 1)

    def hop_right(c):
        return pltpu.make_async_remote_copy(
            src_ref=out_r.at[c],
            dst_ref=in_r.at[c],
            send_sem=send_r.at[c],
            recv_sem=recv_r.at[c],
            device_id={"ctx": lax.rem(me + 1, n)},
            device_id_type=pl.DeviceIdType.MESH,
        )

    def hop_left(c):
        return pltpu.make_async_remote_copy(
            src_ref=out_l.at[c],
            dst_ref=in_l.at[c],
            send_sem=send_l.at[c],
            recv_sem=recv_l.at[c],
            device_id={"ctx": lax.rem(me + n - 1, n)},
            device_id_type=pl.DeviceIdType.MESH,
        )

    def stored_chunk(c):
        value = own[c, 0]
        for e in range(1, own.shape[1]):
            value = jnp.where(chosen == e, own[c, e], value)
        return value

    def relay(t):
        @pl.when(t < count)
        def _():
            own_copy(own.at[t], t).wait()

        right = t - me * LAG

        @pl.when((right >= 0) & (right < count))
        def _():
            @pl.when(me == 0)
            def _():
                out_r[right] = stored_chunk(right)

            @pl.when(me > 0)
            def _():
                hop_right(right).wait_recv()
                out_r[right] = jnp.where(is_source, stored_chunk(right), in_r[right])

            @pl.when(me < n - 1)
            def _():
                hop_right(right).start()

        left = t - (n - 1 - me) * LAG

        @pl.when((left >= 0) & (left < count))
        def _():
            @pl.when(me == n - 1)
            def _():
                out_l[left] = stored_chunk(left)

            @pl.when(me < n - 1)
            def _():
                hop_left(left).wait_recv()
                out_l[left] = jnp.where(is_source, stored_chunk(left), in_l[left])

            @pl.when(me > 0)
            def _():
                hop_left(left).start()

        done = t - fill

        @pl.when(done >= 0)
        def _():
            final[done] = jnp.where(from_left, out_r[done], out_l[done])

    def relay_range(start, stop):
        def one(t, _):
            relay(t)
            return 0

        lax.fori_loop(start, stop, one, 0)

    def tp_copy(src, dst, send, recv, d, sem):
        return pltpu.make_async_remote_copy(
            src_ref=src,
            dst_ref=dst,
            send_sem=send.at[d],
            recv_sem=recv.at[sem],
            device_id={"tp": lax.rem(lane + d, tp)},
            device_id_type=pl.DeviceIdType.MESH,
        )

    def row_share(j):
        return pl.ds(pl.multiple_of(j * share, share), share)

    def each_peer(fn):
        def one(d, _):
            fn(d, lax.rem(lane + d, tp))
            return 0

        lax.fori_loop(1, tp, one, 0)

    def scatter_start(src, buf, send, recv):
        each_peer(
            lambda d, j: tp_copy(
                src.at[row_share(j)], buf.at[lane], send, recv, d, lane
            ).start()
        )
        buf[lane] = src[row_share(lane)]

    def scatter_wait(src, buf, send, recv):
        each_peer(
            lambda d, j: tp_copy(
                src.at[row_share(j)], buf.at[j], send, recv, d, j
            ).wait()
        )
        return jnp.sum(buf[...], axis=0)

    def gather_start(value, buf, send, recv):
        mine = buf.at[row_share(lane)]
        mine[...] = value.astype(buf.dtype)
        each_peer(lambda d, j: tp_copy(mine, mine, send, recv, d, lane).start())

    def gather_wait(buf, send, recv):
        each_peer(
            lambda d, j: tp_copy(
                buf.at[row_share(lane)], buf.at[row_share(j)], send, recv, d, j
            ).wait()
        )

    relay_range(0, fill)
    blocks = order_ref.shape[0]
    block_rows = rows * n // blocks
    per_device = blocks // n
    token = lax.broadcasted_iota(jnp.int32, (rows, HEAD_SIZE), 0)
    stored = jnp.zeros((rows, HEAD_SIZE), jnp.int32)
    for b in range(per_device):
        stored = jnp.where(
            token // block_rows == b, order_ref[me * per_device + b], stored
        )
    position = stored * block_rows + token % block_rows
    angle = position.astype(jnp.float32) * frequency_ref[...]
    half = lax.broadcasted_iota(jnp.int32, (rows, HEAD_SIZE), 1) < HEAD_SIZE // 2
    cosine[...] = jnp.cos(angle)
    sine_all = jnp.sin(angle)
    sine[...] = jnp.where(half, -sine_all, sine_all)
    key = lax.broadcasted_iota(jnp.int32, (rows, block_rows * 2), 1)
    query_position = jnp.concatenate(
        [position] * (block_rows * 2 // HEAD_SIZE), axis=1
    )
    for b in range(0, blocks, 2):
        key_position = (
            jnp.where(key < block_rows, order_ref[b], order_ref[b + 1]) * block_rows
            + key % block_rows
        )
        bias[:, b * block_rows : (b + 2) * block_rows] = jnp.where(
            key_position <= query_position, 0.0, NEG_BIG
        )
    partial[...] = jnp.zeros_like(partial)
    partial2[...] = jnp.zeros_like(partial2)
    base_copies[0].wait()

    def down_step(k, _):
        for r in range(n_down):
            relay(fill + k * n_down + r)
        weight = final[pl.ds(k * n_down, n_down)].reshape(n_down * rank, cw)
        partial[:, : n_down * rank] += lax.dot_general(
            hidden[:, cols(k)], weight, NT, preferred_element_type=jnp.float32
        )
        return 0

    lax.fori_loop(0, parts, down_step, 0)
    t = fill + first_k
    scatter_start(partial, rs_buf, rs_send, rs_recv)
    relay_range(t, t + 4)
    gather_start(
        scatter_wait(partial, rs_buf, rs_send, rs_recv), rank_low, ag_send, ag_recv
    )
    relay_range(t + 4, t + 8)
    for copy in base_copies[1:]:
        copy.wait()
    gather_wait(rank_low, ag_send, ag_recv)

    def rotate(values):
        return values * cosine[...] + pltpu.roll(values, HEAD_SIZE // 2, 1) * sine[...]

    low = rank_low[...]
    keys = base_k[...].astype(jnp.float32) + jnp.dot(
        low[:, rank : 2 * rank], final[first_k], preferred_element_type=jnp.float32
    )
    values = base_v[...].astype(jnp.float32) + jnp.dot(
        low[:, 2 * rank : 3 * rank],
        final[first_k + 1],
        preferred_element_type=jnp.float32,
    )
    for g in range(groups):
        span = slice(g * HEAD_SIZE, (g + 1) * HEAD_SIZE)
        kv_all[me, g] = rotate(keys[:, span]).astype(jnp.bfloat16)
        kv_all[me, groups + g] = values[:, span].astype(jnp.bfloat16)

    def kv_copy(d, place):
        return pltpu.make_async_remote_copy(
            src_ref=kv_all.at[me],
            dst_ref=kv_all.at[place],
            send_sem=kv_send.at[d],
            recv_sem=kv_recv.at[place],
            device_id={"ctx": lax.rem(me + d, n)},
            device_id_type=pl.DeviceIdType.MESH,
        )

    def kv_start(d, _):
        kv_copy(d, me).start()
        return 0

    def kv_wait(d, _):
        kv_copy(d, lax.rem(me + d, n)).wait()
        return 0

    lax.fori_loop(1, n, kv_start, 0)

    low_q = low[:, :rank]

    def query_step(j, _):
        relay(t + 8 + j)
        adapted_q = base_q[:, cols(j)].astype(jnp.float32) + jnp.dot(
            low_q, final[first_q + j], preferred_element_type=jnp.float32
        )
        for h in range(heads_per_chunk):
            span = slice(h * HEAD_SIZE, (h + 1) * HEAD_SIZE)
            queries[j, :, span] = rotate(adapted_q[:, span]).astype(jnp.bfloat16)
        return 0

    lax.fori_loop(0, parts, query_step, 0)
    relay_range(t + 8 + parts, fill + first_ou)
    lax.fori_loop(1, n, kv_wait, 0)

    def head_step(j, _):
        relay(fill + first_ou + j)
        for h in range(heads_per_chunk):
            span = slice(h * HEAD_SIZE, (h + 1) * HEAD_SIZE)
            group = (j * heads_per_chunk + h) // group_size
            key_block = kv_all[:, group].reshape(n * rows, HEAD_SIZE)
            value_block = kv_all[:, groups + group].reshape(n * rows, HEAD_SIZE)
            scores = (
                lax.dot_general(
                    queries[j, :, span], key_block, NT, preferred_element_type=jnp.float32
                )
                * HEAD_SIZE ** (-0.5)
                + bias[...]
            )
            raw = jnp.exp(scores - jnp.max(scores, axis=1, keepdims=True))
            totals = jnp.sum(raw, axis=1, keepdims=True)
            mixed = jnp.dot(
                raw.astype(jnp.bfloat16), value_block, preferred_element_type=jnp.float32
            )
            place = pl.ds(pl.multiple_of(j * cw + h * HEAD_SIZE, HEAD_SIZE), HEAD_SIZE)
            attended_ref[:, place] = (mixed / totals).astype(jnp.bfloat16)
        partial2[:, :rank] += lax.dot_general(
            attended_ref[:, cols(j)],
            final[first_od + j],
            NT,
            preferred_element_type=jnp.float32,
        )
        return 0

    lax.fori_loop(0, parts, head_step, 0)
    scatter_start(partial2, rs_buf2, rs2_send, rs2_recv)
    gather_start(
        scatter_wait(partial2, rs_buf2, rs2_send, rs2_recv), out_low, ag2_send, ag2_recv
    )

    def drain(c, _):
        @pl.when(me < n - 1)
        def _():
            hop_right(c).wait_send()

        @pl.when(me > 0)
        def _():
            hop_left(c).wait_send()

        return 0

    lax.fori_loop(0, count, drain, 0)
    gather_wait(out_low, ag2_send, ag2_recv)
    outer = out_low[:, :rank]

    def up_step(j, _):
        adapted_ref[:, cols(j)] = jnp.dot(
            outer, final[first_ou + j], preferred_element_type=jnp.float32
        ).astype(jnp.bfloat16)
        return 0

    lax.fori_loop(0, parts, up_step, 0)


def shards(
    n,
    tp,
    hidden,
    base_query_rows,
    base_key_rows,
    base_value_rows,
    stored_block_order,
    version,
    publisher,
    adapter_down_weight,
    adapter_up_query,
    adapter_up_key_value,
    output_down_weight,
    output_up_weight,
):
    rows, width = hidden.shape
    versions, rank = adapter_up_query.shape[1:3]
    kv_width = base_key_rows.shape[1]
    groups = kv_width // HEAD_SIZE
    cw = width // PARTS
    count = adapter_down_weight.shape[2] // rank * PARTS + 2 + 3 * PARTS
    half = np.arange(HEAD_SIZE // 2, dtype=np.float32) * np.float32(2.0) / np.float32(HEAD_SIZE)
    frequency = np.power(np.float32(500000.0), -half).astype(np.float32)
    frequency = jnp.asarray(np.concatenate([frequency, frequency])[None, :])
    bf16, f32 = jnp.bfloat16, jnp.float32
    chunk = pltpu.VMEM((count, rank, cw), bf16)
    dma = pltpu.SemaphoreType.DMA
    share = rows // tp
    smem = pl.BlockSpec(memory_space=pltpu.SMEM)
    vmem = pl.BlockSpec(memory_space=pltpu.VMEM)
    hbm = pl.BlockSpec(memory_space=pltpu.HBM)
    out = jax.ShapeDtypeStruct((rows, width), bf16)
    return pl.pallas_call(
        functools.partial(kernel, n, tp, width // kv_width),
        out_shape=(out, out),
        in_specs=[smem] * 3 + [vmem] + [hbm] * 9,
        out_specs=(vmem, vmem),
        scratch_shapes=[
            pltpu.VMEM((rows, width), bf16),
            pltpu.VMEM((rows, width), bf16),
            pltpu.VMEM((rows, kv_width), bf16),
            pltpu.VMEM((rows, kv_width), bf16),
            pltpu.VMEM((count, versions, rank, cw), bf16),
            chunk,
            chunk,
            chunk,
            chunk,
            chunk,
            pltpu.VMEM((PARTS, rows, cw), bf16),
            pltpu.VMEM((n, 2 * groups, rows, HEAD_SIZE), bf16),
            pltpu.VMEM((rows, n * rows), f32),
            pltpu.VMEM((rows, HEAD_SIZE), f32),
            pltpu.VMEM((rows, HEAD_SIZE), f32),
            pltpu.VMEM((rows, 2 * HEAD_SIZE), f32),
            pltpu.VMEM((tp, share, 2 * HEAD_SIZE), f32),
            pltpu.VMEM((rows, 2 * HEAD_SIZE), bf16),
            pltpu.VMEM((rows, HEAD_SIZE), f32),
            pltpu.VMEM((tp, share, HEAD_SIZE), f32),
            pltpu.VMEM((rows, HEAD_SIZE), bf16),
            dma((count,)),
            dma((4,)),
            dma((count,)),
            dma((count,)),
            dma((count,)),
            dma((count,)),
            dma((n,)),
            dma((n,)),
        ]
        + [dma((tp,))] * 8,
        compiler_params=pltpu.CompilerParams(
            collective_id=0, has_side_effects=True, vmem_limit_bytes=48 * 1024 * 1024
        ),
    )(
        stored_block_order,
        version,
        publisher,
        frequency,
        hidden,
        base_query_rows,
        base_key_rows,
        base_value_rows,
        adapter_down_weight,
        adapter_up_query,
        adapter_up_key_value,
        output_down_weight,
        output_up_weight,
    )


def solution(mesh):
    placed = (
        P(("groups", "ctx"), "tp"),
        P(("groups", "ctx"), "tp"),
        P(("groups", "ctx"), "tp"),
        P(("groups", "ctx"), "tp"),
        P("groups"),
        P("groups"),
        P("groups"),
        P("ctx", None, None, "tp"),
        P("ctx", None, None, "tp"),
        P("ctx", None, None, None, "tp"),
        P("ctx", None, None, "tp"),
        P("ctx", None, None, "tp"),
    )
    return jax.shard_map(
        functools.partial(shards, mesh.shape["ctx"], mesh.shape["tp"]),
        mesh=mesh,
        in_specs=placed,
        out_specs=(P(("groups", "ctx"), "tp"), P(("groups", "ctx"), "tp")),
        check_vma=False,
    )
```

```python
import functools

import jax
import jax.numpy as jnp
import numpy as np
from jax import lax
from jax.experimental import pallas as pl
from jax.experimental.pallas import tpu as pltpu
from jax.sharding import PartitionSpec as P

HEAD_SIZE = 128
ADAPTER_RANK = 64
NEG_BIG = -1e30
SCALE = HEAD_SIZE**-0.5 * 1.4426950408889634
NT = (((1,), (1,)), ((), ()))
PARTS = 8
LAG = 4


def kernel(
    n,
    tp,
    group_size,
    order_ref,
    version_ref,
    publisher_ref,
    frequency_ref,
    hidden_hbm,
    base_q_hbm,
    base_k_hbm,
    base_v_hbm,
    down_hbm,
    up_q_hbm,
    up_kv_hbm,
    outer_down_hbm,
    outer_up_hbm,
    attended_ref,
    adapted_ref,
    hidden,
    base_q,
    base_k,
    base_v,
    own,
    in_r,
    in_l,
    out_r,
    out_l,
    final,
    queries,
    kv_all,
    bias,
    cosine,
    sine,
    partial,
    rs_buf,
    rank_low,
    partial2,
    rs_buf2,
    out_low,
    own_sem,
    base_sem,
    send_r,
    recv_r,
    send_l,
    recv_l,
    kv_send,
    kv_recv,
    rs_send,
    rs_recv,
    ag_send,
    ag_recv,
    rs2_send,
    rs2_recv,
    ag2_send,
    ag2_recv,
):
    me = lax.axis_index("ctx")
    lane = lax.axis_index("tp")
    count, _, rank, cw = own.shape
    rows, width = hidden.shape
    parts = width // cw
    n_down = down_hbm.shape[2] // rank
    first_k = n_down * parts
    first_q = first_k + 2
    first_od = first_q + parts
    first_ou = first_od + parts
    heads_per_chunk = cw // HEAD_SIZE
    groups = kv_all.shape[1] // 2
    share = rows // tp
    fill = (n - 1) * LAG

    def own_copy(src, c):
        return pltpu.make_async_copy(src, own.at[c], own_sem.at[c])

    def cols(k):
        return pl.ds(pl.multiple_of(k * cw, cw), cw)

    def load_down(k, _):
        for r in range(n_down):
            own_copy(
                down_hbm.at[0, :, pl.ds(r * rank, rank), cols(k)], k * n_down + r
            ).start()
        return 0

    base_copies = [
        pltpu.make_async_copy(src, dst, base_sem.at[i])
        for i, (src, dst) in enumerate(
            [(hidden_hbm, hidden), (base_q_hbm, base_q), (base_k_hbm, base_k), (base_v_hbm, base_v)]
        )
    ]

    barrier = pltpu.get_barrier_semaphore()

    def greet(axis, own_index, size):
        def one(d, _):
            pl.semaphore_signal(
                barrier,
                inc=1,
                device_id={axis: lax.rem(own_index + d, size)},
                device_id_type=pl.DeviceIdType.MESH,
            )
            return 0

        lax.fori_loop(1, size, one, 0)

    greet("ctx", me, n)
    greet("tp", lane, tp)

    load_down(0, 0)
    base_copies[0].start()
    lax.fori_loop(1, parts, load_down, 0)
    for c in range(2):
        own_copy(up_kv_hbm.at[0, :, c], first_k + c).start()

    def load_wide(k, _):
        own_copy(up_q_hbm.at[0, :, :, cols(k)], first_q + k).start()
        own_copy(outer_down_hbm.at[0, :, :, cols(k)], first_od + k).start()
        own_copy(outer_up_hbm.at[0, :, :, cols(k)], first_ou + k).start()
        return 0

    lax.fori_loop(0, parts, load_wide, 0)
    for copy in base_copies[1:]:
        copy.start()

    source = publisher_ref[0]
    chosen = version_ref[source]
    is_source = source == me
    from_left = source <= me

    pl.semaphore_wait(barrier, n - 1 + tp - 1)

    def hop_right(c):
        return pltpu.make_async_remote_copy(
            src_ref=out_r.at[c],
            dst_ref=in_r.at[c],
            send_sem=send_r.at[c],
            recv_sem=recv_r.at[c],
            device_id={"ctx": lax.rem(me + 1, n)},
            device_id_type=pl.DeviceIdType.MESH,
        )

    def hop_left(c):
        return pltpu.make_async_remote_copy(
            src_ref=out_l.at[c],
            dst_ref=in_l.at[c],
            send_sem=send_l.at[c],
            recv_sem=recv_l.at[c],
            device_id={"ctx": lax.rem(me + n - 1, n)},
            device_id_type=pl.DeviceIdType.MESH,
        )

    def stored_chunk(c):
        value = own[c, 0]
        for e in range(1, own.shape[1]):
            value = jnp.where(chosen == e, own[c, e], value)
        return value

    def relay(t):
        @pl.when(t < count)
        def _():
            own_copy(own.at[t], t).wait()

        right = t - me * LAG

        @pl.when((right >= 0) & (right < count))
        def _():
            @pl.when(me == 0)
            def _():
                out_r[right] = stored_chunk(right)

            @pl.when(me > 0)
            def _():
                hop_right(right).wait_recv()
                out_r[right] = jnp.where(is_source, stored_chunk(right), in_r[right])

            @pl.when(me < n - 1)
            def _():
                hop_right(right).start()

        left = t - (n - 1 - me) * LAG

        @pl.when((left >= 0) & (left < count))
        def _():
            @pl.when(me == n - 1)
            def _():
                out_l[left] = stored_chunk(left)

            @pl.when(me < n - 1)
            def _():
                hop_left(left).wait_recv()
                out_l[left] = jnp.where(is_source, stored_chunk(left), in_l[left])

            @pl.when(me > 0)
            def _():
                hop_left(left).start()

        done = t - fill

        @pl.when(done >= 0)
        def _():
            final[done] = jnp.where(from_left, out_r[done], out_l[done])

    def relay_range(start, stop):
        def one(t, _):
            relay(t)
            return 0

        lax.fori_loop(start, stop, one, 0)

    def tp_copy(src, dst, send, recv, d, sem):
        return pltpu.make_async_remote_copy(
            src_ref=src,
            dst_ref=dst,
            send_sem=send.at[d],
            recv_sem=recv.at[sem],
            device_id={"tp": lax.rem(lane + d, tp)},
            device_id_type=pl.DeviceIdType.MESH,
        )

    def row_share(j):
        return pl.ds(pl.multiple_of(j * share, share), share)

    def each_peer(fn):
        def one(d, _):
            fn(d, lax.rem(lane + d, tp))
            return 0

        lax.fori_loop(1, tp, one, 0)

    def scatter_start(src, buf, send, recv):
        each_peer(
            lambda d, j: tp_copy(
                src.at[row_share(j)], buf.at[lane], send, recv, d, lane
            ).start()
        )
        buf[lane] = src[row_share(lane)]

    def scatter_wait(src, buf, send, recv):
        each_peer(
            lambda d, j: tp_copy(
                src.at[row_share(j)], buf.at[j], send, recv, d, j
            ).wait()
        )
        return jnp.sum(buf[...], axis=0)

    def gather_start(value, buf, send, recv):
        mine = buf.at[row_share(lane)]
        mine[...] = value.astype(buf.dtype)
        each_peer(lambda d, j: tp_copy(mine, mine, send, recv, d, lane).start())

    def gather_wait(buf, send, recv):
        each_peer(
            lambda d, j: tp_copy(
                buf.at[row_share(lane)], buf.at[row_share(j)], send, recv, d, j
            ).wait()
        )

    relay_range(0, fill)
    blocks = order_ref.shape[0]
    block_rows = rows * n // blocks
    per_device = blocks // n
    token = lax.broadcasted_iota(jnp.int32, (rows, HEAD_SIZE), 0)
    stored = jnp.zeros((rows, HEAD_SIZE), jnp.int32)
    for b in range(per_device):
        stored = jnp.where(
            token // block_rows == b, order_ref[me * per_device + b], stored
        )
    position = stored * block_rows + token % block_rows
    angle = position.astype(jnp.float32) * frequency_ref[...]
    half = lax.broadcasted_iota(jnp.int32, (rows, HEAD_SIZE), 1) < HEAD_SIZE // 2
    cosine[...] = jnp.cos(angle)
    sine_all = jnp.sin(angle)
    sine[...] = jnp.where(half, -sine_all, sine_all)
    key = lax.broadcasted_iota(jnp.int32, (rows, block_rows * 2), 1)
    query_position = jnp.concatenate(
        [position] * (block_rows * 2 // HEAD_SIZE), axis=1
    )
    for b in range(0, blocks, 2):
        key_position = (
            jnp.where(key < block_rows, order_ref[b], order_ref[b + 1]) * block_rows
            + key % block_rows
        )
        bias[:, b * block_rows : (b + 2) * block_rows] = jnp.where(
            key_position <= query_position, 0.0, NEG_BIG
        )
    partial[...] = jnp.zeros_like(partial)
    partial2[...] = jnp.zeros_like(partial2)
    base_copies[0].wait()

    def down_step(k, _):
        for r in range(n_down):
            relay(fill + k * n_down + r)
        weight = final[pl.ds(k * n_down, n_down)].reshape(n_down * rank, cw)
        partial[:, : n_down * rank] += lax.dot_general(
            hidden[:, cols(k)], weight, NT, preferred_element_type=jnp.float32
        )
        return 0

    lax.fori_loop(0, parts, down_step, 0)
    t = fill + first_k
    scatter_start(partial, rs_buf, rs_send, rs_recv)
    relay_range(t, t + 4)
    gather_start(
        scatter_wait(partial, rs_buf, rs_send, rs_recv), rank_low, ag_send, ag_recv
    )
    relay_range(t + 4, t + 8)
    for copy in base_copies[1:]:
        copy.wait()
    gather_wait(rank_low, ag_send, ag_recv)

    def rotate(values):
        return values * cosine[...] + pltpu.roll(values, HEAD_SIZE // 2, 1) * sine[...]

    low = rank_low[...]
    keys = base_k[...].astype(jnp.float32) + jnp.dot(
        low[:, rank : 2 * rank], final[first_k], preferred_element_type=jnp.float32
    )
    values = base_v[...].astype(jnp.float32) + jnp.dot(
        low[:, 2 * rank : 3 * rank],
        final[first_k + 1],
        preferred_element_type=jnp.float32,
    )
    for g in range(groups):
        span = slice(g * HEAD_SIZE, (g + 1) * HEAD_SIZE)
        kv_all[me, g] = rotate(keys[:, span]).astype(jnp.bfloat16)
        kv_all[me, groups + g] = values[:, span].astype(jnp.bfloat16)

    def kv_copy(d, place):
        return pltpu.make_async_remote_copy(
            src_ref=kv_all.at[me],
            dst_ref=kv_all.at[place],
            send_sem=kv_send.at[d],
            recv_sem=kv_recv.at[place],
            device_id={"ctx": lax.rem(me + d, n)},
            device_id_type=pl.DeviceIdType.MESH,
        )

    def kv_start(d, _):
        kv_copy(d, me).start()
        return 0

    def kv_wait(d, _):
        kv_copy(d, lax.rem(me + d, n)).wait()
        return 0

    lax.fori_loop(1, n, kv_start, 0)

    low_q = low[:, :rank]

    def query_step(j, _):
        relay(t + 8 + j)
        adapted_q = base_q[:, cols(j)].astype(jnp.float32) + jnp.dot(
            low_q, final[first_q + j], preferred_element_type=jnp.float32
        )
        for h in range(heads_per_chunk):
            span = slice(h * HEAD_SIZE, (h + 1) * HEAD_SIZE)
            queries[j * heads_per_chunk + h] = rotate(adapted_q[:, span]).astype(jnp.bfloat16)
        return 0

    lax.fori_loop(0, parts, query_step, 0)
    relay_range(t + 8 + parts, fill + first_ou)
    lax.fori_loop(1, n, kv_wait, 0)

    heads = width // HEAD_SIZE
    batch = min(4, group_size)
    batches = heads // batch
    relays = -(-parts // batches)
    chunks = batch // heads_per_chunk

    def head_step(i, _):
        for r in range(relays):
            @pl.when(i * relays + r < parts)
            def _():
                relay(fill + first_ou + i * relays + r)

        group = i * batch // group_size
        key_block = kv_all[:, group].reshape(n * rows, HEAD_SIZE)
        value_block = kv_all[:, groups + group].reshape(n * rows, HEAD_SIZE)
        query_block = queries[pl.ds(i * batch, batch)].reshape(batch * rows, HEAD_SIZE)
        scores = lax.dot_general(
            query_block, key_block, NT, preferred_element_type=jnp.float32
        ).reshape(batch, rows, n * rows)
        scores = scores + bias[...][None]
        raw = jnp.exp2((scores - jnp.max(scores, axis=2, keepdims=True)) * SCALE)
        totals = jnp.sum(raw, axis=2, keepdims=True)
        mixed = jnp.dot(
            raw.astype(jnp.bfloat16).reshape(batch * rows, n * rows),
            value_block,
            preferred_element_type=jnp.float32,
        ).reshape(batch, rows, HEAD_SIZE)
        mixed = (mixed / totals).astype(jnp.bfloat16)
        for h in range(batch):
            place = pl.ds(pl.multiple_of((i * batch + h) * HEAD_SIZE, HEAD_SIZE), HEAD_SIZE)
            attended_ref[:, place] = mixed[h]
        added = jnp.zeros((rows, rank), jnp.float32)
        for c in range(chunks):
            added += lax.dot_general(
                attended_ref[:, cols(i * chunks + c)],
                final[first_od + i * chunks + c],
                NT,
                preferred_element_type=jnp.float32,
            )
        partial2[:, :rank] += added
        return 0

    lax.fori_loop(0, batches, head_step, 0)
    scatter_start(partial2, rs_buf2, rs2_send, rs2_recv)
    gather_start(
        scatter_wait(partial2, rs_buf2, rs2_send, rs2_recv), out_low, ag2_send, ag2_recv
    )

    def drain(c, _):
        @pl.when(me < n - 1)
        def _():
            hop_right(c).wait_send()

        @pl.when(me > 0)
        def _():
            hop_left(c).wait_send()

        return 0

    lax.fori_loop(0, count, drain, 0)
    gather_wait(out_low, ag2_send, ag2_recv)
    outer = out_low[:, :rank]

    for j in range(parts):
        adapted_ref[:, j * cw : (j + 1) * cw] = jnp.dot(
            outer, final[first_ou + j], preferred_element_type=jnp.float32
        ).astype(jnp.bfloat16)


def shards(
    n,
    tp,
    hidden,
    base_query_rows,
    base_key_rows,
    base_value_rows,
    stored_block_order,
    version,
    publisher,
    adapter_down_weight,
    adapter_up_query,
    adapter_up_key_value,
    output_down_weight,
    output_up_weight,
):
    rows, width = hidden.shape
    versions, rank = adapter_up_query.shape[1:3]
    kv_width = base_key_rows.shape[1]
    groups = kv_width // HEAD_SIZE
    cw = width // PARTS
    count = adapter_down_weight.shape[2] // rank * PARTS + 2 + 3 * PARTS
    half = np.arange(HEAD_SIZE // 2, dtype=np.float32) * np.float32(2.0) / np.float32(HEAD_SIZE)
    frequency = np.power(np.float32(500000.0), -half).astype(np.float32)
    frequency = jnp.asarray(np.concatenate([frequency, frequency])[None, :])
    bf16, f32 = jnp.bfloat16, jnp.float32
    chunk = pltpu.VMEM((count, rank, cw), bf16)
    dma = pltpu.SemaphoreType.DMA
    share = rows // tp
    smem = pl.BlockSpec(memory_space=pltpu.SMEM)
    vmem = pl.BlockSpec(memory_space=pltpu.VMEM)
    hbm = pl.BlockSpec(memory_space=pltpu.HBM)
    out = jax.ShapeDtypeStruct((rows, width), bf16)
    return pl.pallas_call(
        functools.partial(kernel, n, tp, width // kv_width),
        out_shape=(out, out),
        in_specs=[smem] * 3 + [vmem] + [hbm] * 9,
        out_specs=(vmem, vmem),
        scratch_shapes=[
            pltpu.VMEM((rows, width), bf16),
            pltpu.VMEM((rows, width), bf16),
            pltpu.VMEM((rows, kv_width), bf16),
            pltpu.VMEM((rows, kv_width), bf16),
            pltpu.VMEM((count, versions, rank, cw), bf16),
            chunk,
            chunk,
            chunk,
            chunk,
            chunk,
            pltpu.VMEM((width // HEAD_SIZE, rows, HEAD_SIZE), bf16),
            pltpu.VMEM((n, 2 * groups, rows, HEAD_SIZE), bf16),
            pltpu.VMEM((rows, n * rows), f32),
            pltpu.VMEM((rows, HEAD_SIZE), f32),
            pltpu.VMEM((rows, HEAD_SIZE), f32),
            pltpu.VMEM((rows, 2 * HEAD_SIZE), f32),
            pltpu.VMEM((tp, share, 2 * HEAD_SIZE), f32),
            pltpu.VMEM((rows, 2 * HEAD_SIZE), bf16),
            pltpu.VMEM((rows, HEAD_SIZE), f32),
            pltpu.VMEM((tp, share, HEAD_SIZE), f32),
            pltpu.VMEM((rows, HEAD_SIZE), bf16),
            dma((count,)),
            dma((4,)),
            dma((count,)),
            dma((count,)),
            dma((count,)),
            dma((count,)),
            dma((n,)),
            dma((n,)),
        ]
        + [dma((tp,))] * 8,
        compiler_params=pltpu.CompilerParams(
            collective_id=0, has_side_effects=True, vmem_limit_bytes=63 * 1024 * 1024
        ),
    )(
        stored_block_order,
        version,
        publisher,
        frequency,
        hidden,
        base_query_rows,
        base_key_rows,
        base_value_rows,
        adapter_down_weight,
        adapter_up_query,
        adapter_up_key_value,
        output_down_weight,
        output_up_weight,
    )


def solution(mesh):
    placed = (
        P(("groups", "ctx"), "tp"),
        P(("groups", "ctx"), "tp"),
        P(("groups", "ctx"), "tp"),
        P(("groups", "ctx"), "tp"),
        P("groups"),
        P("groups"),
        P("groups"),
        P("ctx", None, None, "tp"),
        P("ctx", None, None, "tp"),
        P("ctx", None, None, None, "tp"),
        P("ctx", None, None, "tp"),
        P("ctx", None, None, "tp"),
    )
    return jax.shard_map(
        functools.partial(shards, mesh.shape["ctx"], mesh.shape["tp"]),
        mesh=mesh,
        in_specs=placed,
        out_specs=(P(("groups", "ctx"), "tp"), P(("groups", "ctx"), "tp")),
        check_vma=False,
    )
```
